32 devices in a mesh: group: 2 (over y), section: 4 (over z), ctx: 2 (over core), head: 2 (over x).
Axes of the slice: x: 2, y: 2, z: 4, core: 2. Of those that a mesh axis runs over, the one named last changes fastest.
Arguments:
- queries: bfloat16 [2048, 48, 128], P(('group', 'section'), 'head'), parts along dimension 0, may hold values from -6 to 6
- slice_kv: bfloat16 [2048, 2, 128], P(('group', 'section')), parts along dimension 0, may hold values from -6 to 6
- cache_keys: bfloat16 [8, 16, 128, 128], P(('group', 'section'), 'ctx'), parts along dimension 0
- cache_values: bfloat16 [8, 16, 128, 128], P(('group', 'section'), 'ctx'), parts along dimension 0, may hold values from -6 to 6
- block_table: int32 [8, 16], P('group'), parts along dimension 0, may hold values from 0 to 15, each once within a row
- slice_index: int32 [8], P('group'), parts along dimension 0, may hold values from 0 to 3, as said below
- out_weight: bfloat16 [48, 128, 6144], P('head', 'section', 'ctx'), may hold values from -0.078125 to 0.078125
Outputs:
- mixed: bfloat16 [2048, 6144], P(('group', 'section'), ('ctx', 'head')), parts along dimension 0
The draws below stay inside these ranges and needn't reach their ends.
There are 2 independent parts, one for each index of `group`. The reference program is written for one: setup_inputs(seed, part) draws one part's arguments, and reference() takes and returns one part's arrays. A program takes and returns all parts, laid end to end along the dimension named above; an argument that names none is the same for every part. Nothing has to cross between parts.
Inputs may be any that keep to these rules, and one draw needn't show every extreme that they name: `slice_index`: every value appears once; the sections s and s + 4 / 2 (for s < 2) hold slice indices that sum to 3.
All inputs are finite; a program needn't handle non-finite values.
Results may differ from the reference program's by a relative error of at most 0.018.
Values may be sent and summed in bfloat16 or wider, within the bound.
A program may use at most 64 MiB of HBM per device.

```python
import jax
import jax.numpy as jnp
from jax import lax

D = 6144
HEADS = 48
HD = 128
BLK = 128
BPS = 4
SECTIONS = 4
POOL = 16
TOKENS = 1024


def draw_cache_keys(key, part):
    full_shape = (SECTIONS, POOL, BLK, HD)
    key_base, key_pick = jax.random.split(jax.random.fold_in(key, 11), 2)
    picked = jax.random.bernoulli(key_pick, 1.0 / 32.0, (SECTIONS, POOL, BLK, 1))
    spread = jnp.where(picked, 3.0, 1.0).astype(jnp.float32)
    normal_part = jax.random.normal(key_base, full_shape, jnp.float32)
    return (spread * normal_part).astype(jnp.bfloat16)


def draw_slice_index(key, part):
    section_count = POOL // BPS
    half_count = section_count // 2
    key_perm, key_coin = jax.random.split(jax.random.fold_in(key, 23))
    values_perm = jax.random.permutation(key_perm, jnp.arange(half_count, dtype=jnp.int32))
    coin_flip = jax.random.randint(key_coin, (half_count,), 0, 2, dtype=jnp.int32)
    left_part = jnp.where(coin_flip == 1, values_perm, section_count - 1 - values_perm)
    right_part = section_count - 1 - left_part
    return jnp.concatenate([left_part, right_part]).astype(jnp.int32)


def block_scale(own_key, extent, pieces, low, high):
    gain = 1.0
    for axis_at, shards_of in pieces:
        steps = jax.random.uniform(jax.random.fold_in(jax.random.fold_in(own_key, 6), axis_at), (shards_of,), jnp.float32, low / len(pieces), high / len(pieces))
        gain = gain * jnp.repeat(jnp.exp(steps), extent[axis_at] // shards_of).reshape((-1,) + (1,) * (len(extent) - 1 - axis_at))
    return gain


def gaussian(stream_key, dims, width, bound, cuts=(), held_as=jnp.bfloat16):
    drawn = jax.random.normal(stream_key, dims, jnp.float32) * width
    if len(cuts) > 0:
        drawn = block_scale(stream_key, dims, cuts, -0.22, 0.18) * drawn
    return jnp.clip(drawn, min=-bound, max=bound).astype(held_as)


def setup_inputs(seed: int = 0, part: int = 0) -> dict:
    splits = jax.random.split(jax.random.key(seed), 8)
    own_keys = jax.random.split(jax.random.fold_in(splits[7], part), 8)
    return {
        "queries": gaussian(own_keys[0], (TOKENS, HEADS, HD), 1.0, 6.0, ((0, 4), (1, 2))),
        "slice_kv": gaussian(own_keys[1], (TOKENS, 2, HD), 1.0, 6.0, ((0, 4),)),
        "cache_keys": draw_cache_keys(jax.random.fold_in(jax.random.fold_in(splits[7], part), 71), part),
        "cache_values": gaussian(own_keys[3], (SECTIONS, POOL, BLK, HD), 1.0, 6.0, ((0, 4), (1, 2))),
        "block_table": jax.vmap(lambda own: jax.random.permutation(own, POOL))(jax.random.split(own_keys[4], SECTIONS)).reshape((SECTIONS, POOL)).astype(jnp.int32),
        "slice_index": draw_slice_index(jax.random.fold_in(jax.random.fold_in(splits[7], part), 71), part),
        "out_weight": gaussian(splits[6], (HEADS, HD, D), (HEADS * HD) ** -0.5, 0.078125, ((0, 2), (1, 4), (2, 2))),
    }


negative_floor = -1e30


def reference(queries, slice_kv, cache_keys, cache_values, block_table, slice_index, out_weight):
    section_count = block_table.shape[0]
    pool_size = block_table.shape[1]
    slice_len = queries.shape[0] // section_count
    head_count = queries.shape[1]
    head_dim = queries.shape[2]
    block_len = cache_keys.shape[2]
    score_scale = 1.0 / (head_dim ** 0.5)
    grouped_queries = queries.reshape(section_count, slice_len, head_count, head_dim)
    grouped_kv = slice_kv.reshape(section_count, slice_len, 2, head_dim)

    def one_section(section_items):
        section_queries, section_kv, section_keys, section_values, table_row, slice_number = section_items
        block_ids = jnp.arange(pool_size, dtype=jnp.int32)
        block_rank = jnp.sum(jnp.where(table_row[None, :] == block_ids[:, None], block_ids[None, :], 0), axis=1)
        active = block_rank < (slice_number + 1) * BPS
        cache_live = jnp.repeat(active, block_len)
        positions = jnp.arange(slice_len, dtype=jnp.int32)
        own_live = positions[None, :] <= positions[:, None]
        visible = jnp.concatenate([jnp.broadcast_to(cache_live[None, :], (slice_len, pool_size * block_len)), own_live], axis=1)
        all_keys = jnp.concatenate([section_keys.reshape(-1, head_dim), section_kv[:, 0]], axis=0).astype(jnp.float32)
        all_values = jnp.concatenate([section_values.reshape(-1, head_dim), section_kv[:, 1]], axis=0).astype(jnp.float32)

        def one_head(head_queries):
            scores = jnp.dot(head_queries.astype(jnp.float32), all_keys.T, precision=lax.Precision.HIGHEST) * score_scale
            masked = jnp.where(visible, scores, negative_floor)
            row_max = jnp.max(masked, axis=1)
            weights = jnp.where(visible, jnp.exp(masked - row_max[:, None]), 0.0)
            norm_sum = jnp.sum(weights, axis=1)
            numerator = jnp.dot(weights.astype(jnp.bfloat16).astype(jnp.float32), all_values, precision=lax.Precision.HIGHEST)
            return (numerator / norm_sum[:, None]).astype(jnp.bfloat16)

        per_head = lax.map(one_head, jnp.swapaxes(section_queries, 0, 1))
        return jnp.swapaxes(per_head, 0, 1)

    attended = lax.map(one_section, (grouped_queries, grouped_kv, cache_keys, cache_values, block_table, slice_index))
    flattened = attended.reshape(section_count * slice_len, head_count * head_dim).astype(jnp.float32)
    projection = out_weight.reshape(head_count * head_dim, -1).astype(jnp.float32)
    mixed = jnp.dot(flattened, projection, precision=lax.Precision.HIGHEST)
    return mixed.astype(jnp.bfloat16)
```

```python
import functools
import math

import jax
import jax.numpy as jnp
import numpy as np
from jax import lax
from jax.experimental import pallas as pl
from jax.experimental.pallas import tpu as pltpu
from jax.sharding import PartitionSpec as P

BPS = 4
FLOOR = -1.5e30
HIDDEN = -3e38
MESH = pl.DeviceIdType.MESH


def live_keys(block_table, slice_index, block_len, local_pool):
    section = lax.axis_index("section")
    table_row = block_table[section]
    block_ids = jnp.arange(table_row.shape[0], dtype=jnp.int32)
    rank = jnp.sum(
        jnp.where(table_row[None, :] == block_ids[:, None], block_ids[None, :], 0), axis=1
    )
    active = rank < (slice_index[section] + 1) * BPS
    mine = lax.dynamic_slice_in_dim(active, lax.axis_index("ctx") * local_pool, local_pool)
    return jnp.repeat(mine, block_len)


def plain(queries, slice_kv, cache_keys, cache_values, block_table, slice_index, out_weight):
    slice_len, heads, hd = queries.shape
    ctx, nctx = lax.axis_index("ctx"), lax.axis_size("ctx")
    nsec = lax.axis_size("section")
    half = slice_len // nctx
    scale = 1.0 / math.sqrt(hd)
    own = lax.dynamic_slice_in_dim(slice_kv, ctx * half, half, 0)
    keys = jnp.concatenate([cache_keys[0].reshape(-1, hd), own[:, 0]], axis=0)
    values = jnp.concatenate([cache_values[0].reshape(-1, hd), own[:, 1]], axis=0)
    live = live_keys(block_table, slice_index, cache_keys.shape[2], cache_keys.shape[1])
    at = ctx * half + jnp.arange(half, dtype=jnp.int32)
    tokens = jnp.arange(slice_len, dtype=jnp.int32)
    visible = jnp.concatenate(
        [
            jnp.broadcast_to(live[None, :], (slice_len, live.shape[0])),
            at[None, :] <= tokens[:, None],
        ],
        axis=1,
    )

    def one_head(q):
        scores = (
            lax.dot_general(q, keys, (((1,), (1,)), ((), ())), preferred_element_type=jnp.float32)
            * scale
        )
        masked = jnp.where(visible, scores, FLOOR)
        top = jnp.max(masked, axis=1)
        weights = jnp.where(visible, jnp.exp(masked - top[:, None]), 0.0)
        acc = jnp.dot(
            weights.astype(jnp.bfloat16), values, preferred_element_type=jnp.float32
        )
        return top, jnp.sum(weights, axis=1), acc

    top, total, acc = lax.map(one_head, jnp.swapaxes(queries, 0, 1))
    factor = jnp.exp(top - lax.pmax(top, "ctx"))
    total = lax.psum(total * factor, "ctx")
    acc = lax.psum((acc * factor[:, :, None]).astype(jnp.bfloat16), "ctx").astype(jnp.float32)
    attended = jnp.swapaxes((acc / total[:, :, None]).astype(jnp.bfloat16), 0, 1)
    pieces = attended.reshape(slice_len, heads, nsec, hd // nsec).transpose(2, 0, 1, 3)
    pieces = lax.all_to_all(pieces, "section", 0, 0)
    projected = jnp.dot(
        pieces.reshape(nsec * slice_len, -1),
        out_weight.reshape(-1, out_weight.shape[2]),
        preferred_element_type=jnp.float32,
    ).astype(jnp.bfloat16)
    summed = lax.psum_scatter(projected, "head", scatter_dimension=1, tiled=True)
    return lax.psum_scatter(summed, "section", scatter_dimension=0, tiled=True)


def kernel(
    dims,
    q_ref, ck_ref, cv_ref, sk_ref, sv_ref, bias_ref, perm_ref, w_ref,
    out_ref,
    w_all, a_all, a_send, acc_own, acc_send, acc_recv, st_own, st_send, st_recv, c_send, c_recv,
    w_local, w_sems, acc_sems, st_sems, z_send, z_recv, x_sems, core_send, core_recv, c_ssem, c_rsem,
):
    slice_len, heads, hd, nsec, stages = dims
    half = slice_len // 2
    per_stage = heads // stages
    group_count = per_stage // nsec
    width = per_stage * hd
    kcols = group_count * hd
    ncols = out_ref.shape[1]
    g, s = lax.axis_index("group"), lax.axis_index("section")
    c, h = lax.axis_index("ctx"), lax.axis_index("head")
    core_peer = (g, s, 1 - c, h)
    x_peer = (g, s, c, 1 - h)

    def sec(k):
        return lax.rem(s + k, nsec)

    def z_peer(k):
        return (g, sec(k), c, h)

    def remote(src, dst, ssem, rsem, to):
        return pltpu.make_async_remote_copy(
            src_ref=src, dst_ref=dst, send_sem=ssem, recv_sem=rsem,
            device_id=to, device_id_type=MESH,
        )

    barrier = pltpu.get_barrier_semaphore()
    for peer in [core_peer, x_peer] + [z_peer(k) for k in range(1, nsec)]:
        pl.semaphore_signal(barrier, inc=1, device_id=peer, device_id_type=MESH)
    pl.semaphore_wait(barrier, nsec + 1)

    def cols_of(which):
        return pl.ds(pl.multiple_of(which * ncols, 128), ncols)

    w_own = pltpu.make_async_copy(w_ref.at[:, cols_of(h)], w_all.at[h], w_local)
    w_own.start()
    w_swap = remote(w_ref.at[:, cols_of(1 - h)], w_all.at[h], w_sems.at[0], w_sems.at[1], x_peer)
    w_swap.start()

    scale = math.log2(math.e) / math.sqrt(hd)
    own_at = pl.ds(pl.multiple_of(c * half, 128), half)
    sends = [w_swap]
    lane = lax.broadcasted_iota(jnp.int32, (half, 128), 1)
    mine = pl.ds(pl.multiple_of(c * half, 128), half)
    theirs = pl.ds(pl.multiple_of((1 - c) * half, 128), half)
    nt = (((1,), (1,)), ((), ()))

    def attend(st):
        st_own[st] = jnp.zeros((half, 128), jnp.float32)
        st_send[st] = jnp.zeros((half, 128), jnp.float32)

        def one(j, rows_at, acc_store, st_ref, row0):
            at = pl.multiple_of((st * per_stage + j) * hd, 128)
            q = q_ref[rows_at, pl.ds(at, hd)]
            t1 = (
                lax.dot_general(q, ck_ref[...], nt, preferred_element_type=jnp.float32) * scale
                + bias_ref[...]
            )
            t2 = (
                lax.dot_general(
                    q, sk_ref[own_at, :], nt, preferred_element_type=jnp.float32
                )
                * scale
            )
            row = lax.broadcasted_iota(jnp.int32, (half, half), 0) + row0
            col = lax.broadcasted_iota(jnp.int32, (half, half), 1) + c * half
            t2 = jnp.where(row >= col, t2, HIDDEN)
            top = jnp.maximum(
                jnp.max(t1, axis=1, keepdims=True), jnp.max(t2, axis=1, keepdims=True)
            )
            top = jnp.maximum(top, FLOOR)
            p1, p2 = jnp.exp2(t1 - top), jnp.exp2(t2 - top)
            total = jnp.sum(p1, axis=1, keepdims=True) + jnp.sum(p2, axis=1, keepdims=True)
            acc = jnp.dot(
                p1.astype(jnp.bfloat16), cv_ref[...], preferred_element_type=jnp.float32
            ) + jnp.dot(
                p2.astype(jnp.bfloat16), sv_ref[own_at, :], preferred_element_type=jnp.float32
            )
            acc_store(pl.multiple_of(j * hd, 128), acc)
            old = st_ref[st]
            st_ref[st] = jnp.where(lane == j, top, jnp.where(lane == 64 + j, total, old))

        def keep(at, acc):
            acc_own[st, :, pl.ds(at, hd)] = acc

        def give(at, acc):
            acc_send[st, :, pl.ds(at, hd)] = acc.astype(jnp.bfloat16)

        def body(j, carry):
            one(j, theirs, give, st_send, (1 - c) * half)
            one(j, mine, keep, st_own, c * half)
            return carry

        lax.fori_loop(0, per_stage, body, 0)
        for buf, got, sems in ((acc_send, acc_recv, acc_sems), (st_send, st_recv, st_sems)):
            copy = remote(buf.at[st], got.at[st], sems.at[0, st], sems.at[1, st], core_peer)
            copy.start()
            sends.append(copy)

    def merge(st):
        for buf, got, sems in ((acc_send, acc_recv, acc_sems), (st_send, st_recv, st_sems)):
            remote(buf.at[st], got.at[st], sems.at[0, st], sems.at[1, st], core_peer).wait_recv()
        stat0, stat1 = st_own[st], st_recv[st]
        done = []
        for j in range(per_stage):
            top0, top1 = stat0[:, j : j + 1], stat1[:, j : j + 1]
            top = jnp.maximum(top0, top1)
            f0, f1 = jnp.exp2(top0 - top), jnp.exp2(top1 - top)
            inv = 1.0 / (stat0[:, 64 + j : 65 + j] * f0 + stat1[:, 64 + j : 65 + j] * f1)
            acc0 = acc_own[st, :, j * hd : (j + 1) * hd]
            acc1 = acc_recv[st, :, j * hd : (j + 1) * hd].astype(jnp.float32)
            done.append(((acc0 * (f0 * inv)) + (acc1 * (f1 * inv))).astype(jnp.bfloat16))
        for i in range(group_count):
            rows = jnp.concatenate(done[i * nsec : (i + 1) * nsec], axis=1)
            moved = jnp.dot(rows, perm_ref[...], preferred_element_type=jnp.float32).astype(
                jnp.bfloat16
            )
            for k in range(nsec):
                a_send[st, k, :, i * hd : (i + 1) * hd] = moved[:, k * hd : (k + 1) * hd]
        a_all[st, h, c, s] = a_send[st, s]
        for k in range(1, nsec):
            copy = remote(
                a_send.at[st, sec(k)], a_all.at[st, h, c, s],
                z_send.at[st, k - 1], z_recv.at[st, k - 1], z_peer(k),
            )
            copy.start()
            sends.append(copy)

    def forward(st):
        for k in range(1, nsec):
            remote(
                a_send.at[st, 0], a_all.at[st, h, c, sec(nsec - k)],
                z_send.at[st, k - 1], z_recv.at[st, k - 1], z_peer(k),
            ).wait_recv()
        held = a_all.at[st, h, c]
        for copy in (
            remote(held, held, x_sems.at[0, st], x_sems.at[1, st], x_peer),
            remote(held, held, core_send.at[st, 0], core_recv.at[st, 0], core_peer),
        ):
            copy.start()
            sends.append(copy)

    def share(st):
        held = a_all.at[st, 1 - h, c]
        remote(held, held, x_sems.at[0, st], x_sems.at[1, st], x_peer).wait_recv()
        copy = remote(held, held, core_send.at[st, 1], core_recv.at[st, 1], core_peer)
        copy.start()
        sends.append(copy)

    for step in range(stages + 3):
        if step < stages:
            attend(step)
        if 1 <= step <= stages:
            merge(step - 1)
        if 2 <= step <= stages + 1:
            forward(step - 2)
        if 3 <= step:
            share(step - 3)

    w_own.wait()
    w_swap_in = remote(w_ref.at[:, cols_of(h)], w_all.at[1 - h], w_sems.at[0], w_sems.at[1], x_peer)
    w_swap_in.wait_recv()
    for st in range(stages):
        for i, which in enumerate((h, 1 - h)):
            held = a_all.at[st, which, 1 - c]
            remote(held, held, core_send.at[st, i], core_recv.at[st, i], core_peer).wait_recv()

    tile = 512 if ncols % 512 == 0 else 128

    def product(which, store):
        def body(n, carry):
            at = pl.ds(pl.multiple_of(n * tile, 128), tile)
            total = jnp.zeros((slice_len, tile), jnp.float32)
            for hh in range(2):
                for st in range(stages):
                    left = a_all[st, hh, :, which].reshape(slice_len, kcols)
                    total += jnp.dot(
                        left,
                        w_all[hh, st * kcols : (st + 1) * kcols, at],
                        preferred_element_type=jnp.float32,
                    )
            store(at, total)
            return carry

        lax.fori_loop(0, ncols // tile, body, 0)

    for k in range(1, nsec):
        def put(at, total, k=k):
            c_send[k - 1, :, at] = total.astype(jnp.bfloat16)

        product(sec(k), put)
        copy = remote(
            c_send.at[k - 1], c_recv.at[k - 1], c_ssem.at[k - 1], c_rsem.at[k - 1], z_peer(k)
        )
        copy.start()
        sends.append(copy)

    for k in range(1, nsec):
        remote(
            c_send.at[k - 1], c_recv.at[k - 1], c_ssem.at[k - 1], c_rsem.at[k - 1], z_peer(k)
        ).wait_recv()

    def finish(at, total):
        for k in range(1, nsec):
            total += c_recv[k - 1, :, at].astype(jnp.float32)
        out_ref[:, at] = total.astype(jnp.bfloat16)

    product(s, finish)
    for copy in sends:
        copy.wait_send()


def fused(queries, slice_kv, cache_keys, cache_values, block_table, slice_index, out_weight):
    slice_len, heads, hd = queries.shape
    nsec = lax.axis_size("section")
    stages = 3
    half = slice_len // 2
    per_stage = heads // stages
    width = per_stage * hd
    kcols = per_stage // nsec * hd
    ncols = out_weight.shape[2] // 2
    depth = out_weight.shape[0] * out_weight.shape[1]
    live = live_keys(block_table, slice_index, cache_keys.shape[2], cache_keys.shape[1])
    bias = jnp.where(live, 0.0, HIDDEN).astype(jnp.float32)[None, :]
    piece = hd // nsec
    perm = np.zeros((nsec, nsec, piece, nsec, nsec, piece), np.float32)
    for head in range(nsec):
        for part in range(nsec):
            for r in range(piece):
                perm[head, part, r, part, head, r] = 1.0
    perm = jnp.asarray(perm.reshape(nsec * hd, nsec * hd), jnp.bfloat16)
    bf16, f32 = jnp.bfloat16, jnp.float32
    dma = pltpu.SemaphoreType.DMA
    vmem = pl.BlockSpec(memory_space=pltpu.VMEM)
    return pl.pallas_call(
        functools.partial(kernel, (slice_len, heads, hd, nsec, stages)),
        out_shape=jax.ShapeDtypeStruct((slice_len, ncols), bf16),
        in_specs=[vmem] * 7 + [pl.BlockSpec(memory_space=pl.ANY)],
        out_specs=vmem,
        scratch_shapes=[
            pltpu.VMEM((2, depth, ncols), bf16),
            pltpu.VMEM((stages, 2, 2, nsec, half, kcols), bf16),
            pltpu.VMEM((stages, nsec, half, kcols), bf16),
            pltpu.VMEM((stages, half, width), f32),
            pltpu.VMEM((stages, half, width), bf16),
            pltpu.VMEM((stages, half, width), bf16),
            pltpu.VMEM((stages, half, 128), f32),
            pltpu.VMEM((stages, half, 128), f32),
            pltpu.VMEM((stages, half, 128), f32),
            pltpu.VMEM((nsec - 1, slice_len, ncols), bf16),
            pltpu.VMEM((nsec - 1, slice_len, ncols), bf16),
            dma,
            dma((2,)),
            dma((2, stages)),
            dma((2, stages)),
            dma((stages, nsec - 1)),
            dma((stages, nsec - 1)),
            dma((2, stages)),
            dma((stages, 2)),
            dma((stages, 2)),
            dma((nsec - 1,)),
            dma((nsec - 1,)),
        ],
        compiler_params=pltpu.CompilerParams(
            collective_id=0, has_side_effects=True, vmem_limit_bytes=52 * 1024 * 1024
        ),
    )(
        queries.reshape(slice_len, heads * hd),
        cache_keys.reshape(-1, hd),
        cache_values.reshape(-1, hd),
        slice_kv[:, 0],
        slice_kv[:, 1],
        bias,
        perm,
        out_weight.reshape(depth, -1),
    )


def on_device(*arrays):
    slice_len, heads, hd = arrays[0].shape
    nsec = lax.axis_size("section")
    fits = (
        lax.axis_size("ctx") == 2
        and lax.axis_size("head") == 2
        and hd == 128
        and slice_len % 256 == 0
        and heads % (3 * nsec) == 0
        and heads // 3 <= 64
        and arrays[6].shape[2] % 256 == 0
    )
    return fused(*arrays) if fits else plain(*arrays)


def solution(mesh):
    placed = (
        P(("group", "section"), "head", None),
        P(("group", "section"), None, None),
        P(("group", "section"), "ctx", None, None),
        P(("group", "section"), "ctx", None, None),
        P("group", None),
        P("group"),
        P("head", "section", "ctx"),
    )
    return jax.shard_map(
        on_device,
        mesh=mesh,
        in_specs=placed,
        out_specs=P(("group", "section"), ("ctx", "head")),
        check_vma=False,
    )
```

```python
import functools
import math

import jax
import jax.numpy as jnp
import numpy as np
from jax import lax
from jax.experimental import pallas as pl
from jax.experimental.pallas import tpu as pltpu
from jax.sharding import PartitionSpec as P

BPS = 4
FLOOR = -1.5e30
HIDDEN = -3e38
MESH = pl.DeviceIdType.MESH


def live_keys(block_table, slice_index, block_len, local_pool):
    section = lax.axis_index("section")
    table_row = block_table[section]
    block_ids = jnp.arange(table_row.shape[0], dtype=jnp.int32)
    rank = jnp.sum(
        jnp.where(table_row[None, :] == block_ids[:, None], block_ids[None, :], 0), axis=1
    )
    active = rank < (slice_index[section] + 1) * BPS
    mine = lax.dynamic_slice_in_dim(active, lax.axis_index("ctx") * local_pool, local_pool)
    return jnp.repeat(mine, block_len)


def plain(queries, slice_kv, cache_keys, cache_values, block_table, slice_index, out_weight):
    slice_len, heads, hd = queries.shape
    ctx, nctx = lax.axis_index("ctx"), lax.axis_size("ctx")
    nsec = lax.axis_size("section")
    half = slice_len // nctx
    scale = 1.0 / math.sqrt(hd)
    own = lax.dynamic_slice_in_dim(slice_kv, ctx * half, half, 0)
    keys = jnp.concatenate([cache_keys[0].reshape(-1, hd), own[:, 0]], axis=0)
    values = jnp.concatenate([cache_values[0].reshape(-1, hd), own[:, 1]], axis=0)
    live = live_keys(block_table, slice_index, cache_keys.shape[2], cache_keys.shape[1])
    at = ctx * half + jnp.arange(half, dtype=jnp.int32)
    tokens = jnp.arange(slice_len, dtype=jnp.int32)
    visible = jnp.concatenate(
        [
            jnp.broadcast_to(live[None, :], (slice_len, live.shape[0])),
            at[None, :] <= tokens[:, None],
        ],
        axis=1,
    )

    def one_head(q):
        scores = (
            lax.dot_general(q, keys, (((1,), (1,)), ((), ())), preferred_element_type=jnp.float32)
            * scale
        )
        masked = jnp.where(visible, scores, FLOOR)
        top = jnp.max(masked, axis=1)
        weights = jnp.where(visible, jnp.exp(masked - top[:, None]), 0.0)
        acc = jnp.dot(
            weights.astype(jnp.bfloat16), values, preferred_element_type=jnp.float32
        )
        return top, jnp.sum(weights, axis=1), acc

    top, total, acc = lax.map(one_head, jnp.swapaxes(queries, 0, 1))
    factor = jnp.exp(top - lax.pmax(top, "ctx"))
    total = lax.psum(total * factor, "ctx")
    acc = lax.psum((acc * factor[:, :, None]).astype(jnp.bfloat16), "ctx").astype(jnp.float32)
    attended = jnp.swapaxes((acc / total[:, :, None]).astype(jnp.bfloat16), 0, 1)
    pieces = attended.reshape(slice_len, heads, nsec, hd // nsec).transpose(2, 0, 1, 3)
    pieces = lax.all_to_all(pieces, "section", 0, 0)
    projected = jnp.dot(
        pieces.reshape(nsec * slice_len, -1),
        out_weight.reshape(-1, out_weight.shape[2]),
        preferred_element_type=jnp.float32,
    ).astype(jnp.bfloat16)
    summed = lax.psum_scatter(projected, "head", scatter_dimension=1, tiled=True)
    return lax.psum_scatter(summed, "section", scatter_dimension=0, tiled=True)


def kernel(
    dims,
    q_ref, ck_ref, cv_ref, sk_ref, sv_ref, bias_ref, perm_ref, w_ref,
    out_ref,
    w_all, a_all, a_send, acc_own, acc_send, acc_recv, st_own, st_send, st_recv,
    right_send, right_recv, left_send, left_recv, kept,
    w_local, w_sems, acc_sems, st_sems, z_send, z_recv, x_sems, core_send, core_recv,
    r_ssem, r_rsem, l_ssem, l_rsem,
):
    slice_len, heads, hd, nsec, stages = dims
    half = slice_len // 2
    per_stage = heads // stages
    group_count = per_stage // nsec
    width = per_stage * hd
    kcols = group_count * hd
    ncols = out_ref.shape[1]
    g, s = lax.axis_index("group"), lax.axis_index("section")
    c, h = lax.axis_index("ctx"), lax.axis_index("head")
    core_peer = (g, s, 1 - c, h)
    twin = (1 - g, s, c, h)
    x_peer = (g, s, c, 1 - h)

    def sec(k):
        return lax.rem(s + k, nsec)

    def z_peer(k):
        return (g, sec(k), c, h)

    def remote(src, dst, ssem, rsem, to):
        return pltpu.make_async_remote_copy(
            src_ref=src, dst_ref=dst, send_sem=ssem, recv_sem=rsem,
            device_id=to, device_id_type=MESH,
        )

    barrier = pltpu.get_barrier_semaphore()
    for peer in [core_peer, x_peer, twin] + [z_peer(k) for k in range(1, nsec)]:
        pl.semaphore_signal(barrier, inc=1, device_id=peer, device_id_type=MESH)
    pl.semaphore_wait(barrier, nsec + 2)

    def cols_of(which):
        return pl.ds(pl.multiple_of(which * ncols, 128), ncols)

    w_own = pltpu.make_async_copy(w_ref.at[:, cols_of(h)], w_all.at[h], w_local)
    w_own.start()
    depth = w_ref.shape[0]
    w_rows = depth // (2 * stages)

    def w_at(which, i):
        return pl.ds(pl.multiple_of(which * (depth // 2) + i * w_rows, 16), w_rows)

    def w_swap(i):
        return remote(
            w_ref.at[w_at(g, i), cols_of(1 - h)], w_all.at[h, w_at(g, i)],
            w_sems.at[0, i], w_sems.at[1, i], x_peer,
        )

    def w_pass(i):
        held = w_all.at[1 - h, w_at(g, i)]
        return remote(held, held, w_sems.at[2, i], w_sems.at[3, i], twin)

    swaps = [w_swap(i) for i in range(stages)]
    for copy in swaps:
        copy.start()

    scale = math.log2(math.e) / math.sqrt(hd)
    own_at = pl.ds(pl.multiple_of(c * half, 128), half)
    sends = list(swaps)
    lane = lax.broadcasted_iota(jnp.int32, (half, 128), 1)
    mine = pl.ds(pl.multiple_of(c * half, 128), half)
    theirs = pl.ds(pl.multiple_of((1 - c) * half, 128), half)
    nt = (((1,), (1,)), ((), ()))

    def attend(st):
        st_own[st] = jnp.zeros((half, 128), jnp.float32)
        st_send[st] = jnp.zeros((half, 128), jnp.float32)

        def one(j, rows_at, acc_store, st_ref, row0):
            at = pl.multiple_of((st * per_stage + j) * hd, 128)
            q = q_ref[rows_at, pl.ds(at, hd)]
            t1 = (
                lax.dot_general(q, ck_ref[...], nt, preferred_element_type=jnp.float32) * scale
                + bias_ref[...]
            )
            t2 = (
                lax.dot_general(
                    q, sk_ref[own_at, :], nt, preferred_element_type=jnp.float32
                )
                * scale
            )
            row = lax.broadcasted_iota(jnp.int32, (half, half), 0) + row0
            col = lax.broadcasted_iota(jnp.int32, (half, half), 1) + c * half
            t2 = jnp.where(row >= col, t2, HIDDEN)
            top = jnp.maximum(
                jnp.max(t1, axis=1, keepdims=True), jnp.max(t2, axis=1, keepdims=True)
            )
            top = jnp.maximum(top, FLOOR)
            p1, p2 = jnp.exp2(t1 - top), jnp.exp2(t2 - top)
            total = jnp.sum(p1, axis=1, keepdims=True) + jnp.sum(p2, axis=1, keepdims=True)
            acc = jnp.dot(
                p1.astype(jnp.bfloat16), cv_ref[...], preferred_element_type=jnp.float32
            ) + jnp.dot(
                p2.astype(jnp.bfloat16), sv_ref[own_at, :], preferred_element_type=jnp.float32
            )
            acc_store(pl.multiple_of(j * hd, 128), acc)
            old = st_ref[st]
            st_ref[st] = jnp.where(lane == j, top, jnp.where(lane == 64 + j, total, old))

        def keep(at, acc):
            acc_own[st, :, pl.ds(at, hd)] = acc

        def give(at, acc):
            acc_send[st, :, pl.ds(at, hd)] = acc.astype(jnp.bfloat16)

        def body(j, carry):
            one(j, theirs, give, st_send, (1 - c) * half)
            one(j, mine, keep, st_own, c * half)
            return carry

        lax.fori_loop(0, per_stage, body, 0)
        for buf, got, sems in ((acc_send, acc_recv, acc_sems), (st_send, st_recv, st_sems)):
            copy = remote(buf.at[st], got.at[st], sems.at[0, st], sems.at[1, st], core_peer)
            copy.start()
            sends.append(copy)

    def merge(st):
        for buf, got, sems in ((acc_send, acc_recv, acc_sems), (st_send, st_recv, st_sems)):
            remote(buf.at[st], got.at[st], sems.at[0, st], sems.at[1, st], core_peer).wait_recv()
        stat0, stat1 = st_own[st], st_recv[st]
        done = []
        for j in range(per_stage):
            top0, top1 = stat0[:, j : j + 1], stat1[:, j : j + 1]
            top = jnp.maximum(top0, top1)
            f0, f1 = jnp.exp2(top0 - top), jnp.exp2(top1 - top)
            inv = 1.0 / (stat0[:, 64 + j : 65 + j] * f0 + stat1[:, 64 + j : 65 + j] * f1)
            acc0 = acc_own[st, :, j * hd : (j + 1) * hd]
            acc1 = acc_recv[st, :, j * hd : (j + 1) * hd].astype(jnp.float32)
            done.append(((acc0 * (f0 * inv)) + (acc1 * (f1 * inv))).astype(jnp.bfloat16))
        for i in range(group_count):
            rows = jnp.concatenate(done[i * nsec : (i + 1) * nsec], axis=1)
            moved = jnp.dot(rows, perm_ref[...], preferred_element_type=jnp.float32).astype(
                jnp.bfloat16
            )
            for k in range(nsec):
                a_send[st, k, :, i * hd : (i + 1) * hd] = moved[:, k * hd : (k + 1) * hd]
        a_all[st, h, c, s] = a_send[st, s]
        for k in range(1, nsec):
            copy = remote(
                a_send.at[st, sec(k)], a_all.at[st, h, c, s],
                z_send.at[st, k - 1], z_recv.at[st, k - 1], z_peer(k),
            )
            copy.start()
            sends.append(copy)

    def forward(st):
        for k in range(1, nsec):
            remote(
                a_send.at[st, 0], a_all.at[st, h, c, sec(nsec - k)],
                z_send.at[st, k - 1], z_recv.at[st, k - 1], z_peer(k),
            ).wait_recv()
        held = a_all.at[st, h, c]
        for copy in (
            remote(held, held, x_sems.at[0, st], x_sems.at[1, st], x_peer),
            remote(held, held, core_send.at[st, 0], core_recv.at[st, 0], core_peer),
        ):
            copy.start()
            sends.append(copy)

    def share(st):
        held = a_all.at[st, 1 - h, c]
        remote(held, held, x_sems.at[0, st], x_sems.at[1, st], x_peer).wait_recv()
        copy = remote(held, held, core_send.at[st, 1], core_recv.at[st, 1], core_peer)
        copy.start()
        sends.append(copy)

    for step in range(stages + 3):
        if step < stages:
            attend(step)
        if 1 <= step <= stages:
            merge(step - 1)
        if 1 <= step <= stages:
            w_swap(step - 1).wait_recv()
            copy = w_pass(step - 1)
            copy.start()
            sends.append(copy)
        if 2 <= step <= stages + 1:
            forward(step - 2)
        if 3 <= step:
            share(step - 3)

    w_own.wait()
    for i in range(stages):
        w_pass(i).wait_recv()
    for st in range(stages):
        for i, which in enumerate((h, 1 - h)):
            held = a_all.at[st, which, 1 - c]
            remote(held, held, core_send.at[st, i], core_recv.at[st, i], core_peer).wait_recv()

    chunk = right_send.shape[2]
    chunks = ncols // chunk

    def product(which, n):
        at = pl.ds(pl.multiple_of(n * chunk, 128), chunk)
        total = jnp.zeros((slice_len, chunk), jnp.float32)
        for hh in range(2):
            for st in range(stages):
                left = a_all[st, hh, :, which].reshape(slice_len, kcols)
                total += jnp.dot(
                    left,
                    w_all[hh, st * kcols : (st + 1) * kcols, at],
                    preferred_element_type=jnp.float32,
                )
        return total

    last = nsec - 1
    ways = (
        (right_send, right_recv, r_ssem, r_rsem, s, 1, lambda i: last - i),
        (left_send, left_recv, l_ssem, l_rsem, last - s, -1, lambda i: i),
    )

    def hop(way, m):
        out, got, ssem, rsem, _, step, _ = way
        to = (g, jnp.clip(s + step, 0, last), c, h)
        return remote(out.at[m], got.at[m], ssem.at[m], rsem.at[m], to)

    def wave(t, carry):
        for way in ways:
            out, got, _, _, behind, _, owner = way
            m = t - behind

            @pl.when((m >= 0) & (m < chunks * (last - behind)))
            def _():
                total = product(owner(m // chunks), m % chunks)

                @pl.when(behind == 0)
                def _():
                    out[m] = total.astype(jnp.bfloat16)

                @pl.when(behind > 0)
                def _():
                    hop(way, m).wait_recv()
                    out[m] = (total + got[m].astype(jnp.float32)).astype(jnp.bfloat16)

                @pl.when(m >= 2)
                def _():
                    hop(way, m - 2).wait_send()

                hop(way, m).start()

        return carry

    lax.fori_loop(0, chunks * last + last, wave, 0)

    for n in range(chunks):
        kept[...] = product(s, n)
        for way in ways:
            got, behind = way[1], way[4]
            m = (last - behind) * chunks + n

            @pl.when(behind > 0)
            def _():
                hop(way, m).wait_recv()
                kept[...] += got[m].astype(jnp.float32)

        out_ref[:, n * chunk : (n + 1) * chunk] = kept[...].astype(jnp.bfloat16)
    for way in ways:
        count = chunks * (last - way[4])
        for back in (2, 1):

            @pl.when(count >= back)
            def _():
                hop(way, count - back).wait_send()

    for copy in sends:
        copy.wait_send()


def fused(queries, slice_kv, cache_keys, cache_values, block_table, slice_index, out_weight):
    slice_len, heads, hd = queries.shape
    nsec = lax.axis_size("section")
    stages = 3
    half = slice_len // 2
    per_stage = heads // stages
    width = per_stage * hd
    kcols = per_stage // nsec * hd
    ncols = out_weight.shape[2] // 2
    depth = out_weight.shape[0] * out_weight.shape[1]
    chunk = 512 if ncols % 512 == 0 else 128
    items = (nsec - 1) * (ncols // chunk)
    live = live_keys(block_table, slice_index, cache_keys.shape[2], cache_keys.shape[1])
    bias = jnp.where(live, 0.0, HIDDEN).astype(jnp.float32)[None, :]
    piece = hd // nsec
    perm = np.zeros((nsec, nsec, piece, nsec, nsec, piece), np.float32)
    for head in range(nsec):
        for part in range(nsec):
            for r in range(piece):
                perm[head, part, r, part, head, r] = 1.0
    perm = jnp.asarray(perm.reshape(nsec * hd, nsec * hd), jnp.bfloat16)
    bf16, f32 = jnp.bfloat16, jnp.float32
    dma = pltpu.SemaphoreType.DMA
    vmem = pl.BlockSpec(memory_space=pltpu.VMEM)
    return pl.pallas_call(
        functools.partial(kernel, (slice_len, heads, hd, nsec, stages)),
        out_shape=jax.ShapeDtypeStruct((slice_len, ncols), bf16),
        in_specs=[vmem] * 7 + [pl.BlockSpec(memory_space=pl.ANY)],
        out_specs=vmem,
        scratch_shapes=[
            pltpu.VMEM((2, depth, ncols), bf16),
            pltpu.VMEM((stages, 2, 2, nsec, half, kcols), bf16),
            pltpu.VMEM((stages, nsec, half, kcols), bf16),
            pltpu.VMEM((stages, half, width), f32),
            pltpu.VMEM((stages, half, width), bf16),
            pltpu.VMEM((stages, half, width), bf16),
            pltpu.VMEM((stages, half, 128), f32),
            pltpu.VMEM((stages, half, 128), f32),
            pltpu.VMEM((stages, half, 128), f32),
            *[pltpu.VMEM((items, slice_len, chunk), bf16)] * 4,
            pltpu.VMEM((slice_len, chunk), f32),
            dma,
            dma((4, stages)),
            dma((2, stages)),
            dma((2, stages)),
            dma((stages, nsec - 1)),
            dma((stages, nsec - 1)),
            dma((2, stages)),
            dma((stages, 2)),
            dma((stages, 2)),
            *[dma((items,))] * 4,
        ],
        compiler_params=pltpu.CompilerParams(
            collective_id=0, has_side_effects=True, vmem_limit_bytes=52 * 1024 * 1024
        ),
    )(
        queries.reshape(slice_len, heads * hd),
        cache_keys.reshape(-1, hd),
        cache_values.reshape(-1, hd),
        slice_kv[:, 0],
        slice_kv[:, 1],
        bias,
        perm,
        out_weight.reshape(depth, -1),
    )


def on_device(*arrays):
    slice_len, heads, hd = arrays[0].shape
    nsec = lax.axis_size("section")
    fits = (
        lax.axis_size("ctx") == 2
        and lax.axis_size("head") == 2
        and lax.axis_size("group") == 2
        and arrays[6].shape[0] * arrays[6].shape[1] % 96 == 0
        and hd == 128
        and slice_len % 256 == 0
        and heads % (3 * nsec) == 0
        and heads // 3 <= 64
        and arrays[6].shape[2] % 256 == 0
    )
    return fused(*arrays) if fits else plain(*arrays)


def solution(mesh):
    placed = (
        P(("group", "section"), "head", None),
        P(("group", "section"), None, None),
        P(("group", "section"), "ctx", None, None),
        P(("group", "section"), "ctx", None, None),
        P("group", None),
        P("group"),
        P("head", "section", "ctx"),
    )
    return jax.shard_map(
        on_device,
        mesh=mesh,
        in_specs=placed,
        out_specs=P(("group", "section"), ("ctx", "head")),
        check_vma=False,
    )
```

```python
import functools
import math

import jax
import jax.numpy as jnp
import numpy as np
from jax import lax
from jax.experimental import pallas as pl
from jax.experimental.pallas import tpu as pltpu
from jax.sharding import PartitionSpec as P

BPS = 4
FLOOR = -1.5e30
HIDDEN = -3e38
MESH = pl.DeviceIdType.MESH


def live_keys(block_table, slice_index, block_len, local_pool):
    section = lax.axis_index("section")
    table_row = block_table[section]
    block_ids = jnp.arange(table_row.shape[0], dtype=jnp.int32)
    rank = jnp.sum(
        jnp.where(table_row[None, :] == block_ids[:, None], block_ids[None, :], 0), axis=1
    )
    active = rank < (slice_index[section] + 1) * BPS
    mine = lax.dynamic_slice_in_dim(active, lax.axis_index("ctx") * local_pool, local_pool)
    return jnp.repeat(mine, block_len)


def plain(queries, slice_kv, cache_keys, cache_values, block_table, slice_index, out_weight):
    slice_len, heads, hd = queries.shape
    ctx, nctx = lax.axis_index("ctx"), lax.axis_size("ctx")
    nsec = lax.axis_size("section")
    half = slice_len // nctx
    scale = 1.0 / math.sqrt(hd)
    own = lax.dynamic_slice_in_dim(slice_kv, ctx * half, half, 0)
    keys = jnp.concatenate([cache_keys[0].reshape(-1, hd), own[:, 0]], axis=0)
    values = jnp.concatenate([cache_values[0].reshape(-1, hd), own[:, 1]], axis=0)
    live = live_keys(block_table, slice_index, cache_keys.shape[2], cache_keys.shape[1])
    at = ctx * half + jnp.arange(half, dtype=jnp.int32)
    tokens = jnp.arange(slice_len, dtype=jnp.int32)
    visible = jnp.concatenate(
        [
            jnp.broadcast_to(live[None, :], (slice_len, live.shape[0])),
            at[None, :] <= tokens[:, None],
        ],
        axis=1,
    )

    def one_head(q):
        scores = (
            lax.dot_general(q, keys, (((1,), (1,)), ((), ())), preferred_element_type=jnp.float32)
            * scale
        )
        masked = jnp.where(visible, scores, FLOOR)
        top = jnp.max(masked, axis=1)
        weights = jnp.where(visible, jnp.exp(masked - top[:, None]), 0.0)
        acc = jnp.dot(
            weights.astype(jnp.bfloat16), values, preferred_element_type=jnp.float32
        )
        return top, jnp.sum(weights, axis=1), acc

    top, total, acc = lax.map(one_head, jnp.swapaxes(queries, 0, 1))
    factor = jnp.exp(top - lax.pmax(top, "ctx"))
    total = lax.psum(total * factor, "ctx")
    acc = lax.psum((acc * factor[:, :, None]).astype(jnp.bfloat16), "ctx").astype(jnp.float32)
    attended = jnp.swapaxes((acc / total[:, :, None]).astype(jnp.bfloat16), 0, 1)
    pieces = attended.reshape(slice_len, heads, nsec, hd // nsec).transpose(2, 0, 1, 3)
    pieces = lax.all_to_all(pieces, "section", 0, 0)
    projected = jnp.dot(
        pieces.reshape(nsec * slice_len, -1),
        out_weight.reshape(-1, out_weight.shape[2]),
        preferred_element_type=jnp.float32,
    ).astype(jnp.bfloat16)
    summed = lax.psum_scatter(projected, "head", scatter_dimension=1, tiled=True)
    return lax.psum_scatter(summed, "section", scatter_dimension=0, tiled=True)


def kernel(
    dims,
    q_ref, ck_ref, cv_ref, sk_ref, sv_ref, bias_ref, perm_ref, w_ref,
    out_ref,
    w_all, a_all, a_send, acc_own, acc_send, acc_recv, st_own, st_send, st_recv,
    right_send, right_recv, left_send, left_recv, kept,
    w_local, w_sems, acc_sems, st_sems, z_send, z_recv, x_sems, core_send, core_recv,
    r_ssem, r_rsem, l_ssem, l_rsem,
):
    slice_len, heads, hd, nsec, stages = dims
    half = slice_len // 2
    rows = half // stages
    tokens = 2 * rows
    group_count = heads // nsec
    ncols = out_ref.shape[1]
    batch = 4
    blocks = heads // batch
    g, s = lax.axis_index("group"), lax.axis_index("section")
    c, h = lax.axis_index("ctx"), lax.axis_index("head")
    core_peer = (g, s, 1 - c, h)
    twin = (1 - g, s, c, h)
    x_peer = (g, s, c, 1 - h)

    def sec(k):
        return lax.rem(s + k, nsec)

    def z_peer(k):
        return (g, sec(k), c, h)

    def remote(src, dst, ssem, rsem, to):
        return pltpu.make_async_remote_copy(
            src_ref=src, dst_ref=dst, send_sem=ssem, recv_sem=rsem,
            device_id=to, device_id_type=MESH,
        )

    barrier = pltpu.get_barrier_semaphore()
    for peer in [core_peer, x_peer, twin] + [z_peer(k) for k in range(1, nsec)]:
        pl.semaphore_signal(barrier, inc=1, device_id=peer, device_id_type=MESH)
    pl.semaphore_wait(barrier, nsec + 2)

    def cols_of(which):
        return pl.ds(pl.multiple_of(which * ncols, 128), ncols)

    w_own = pltpu.make_async_copy(w_ref.at[:, cols_of(h)], w_all.at[h], w_local)
    w_own.start()
    depth = w_ref.shape[0]
    parts = w_sems.shape[1]
    w_rows = depth // (2 * parts)

    def w_at(which, i):
        return pl.ds(pl.multiple_of(which * (depth // 2) + i * w_rows, 16), w_rows)

    def w_swap(i):
        return remote(
            w_ref.at[w_at(g, i), cols_of(1 - h)], w_all.at[h, w_at(g, i)],
            w_sems.at[0, i], w_sems.at[1, i], x_peer,
        )

    def w_pass(i):
        held = w_all.at[1 - h, w_at(g, i)]
        return remote(held, held, w_sems.at[2, i], w_sems.at[3, i], twin)

    swaps = [w_swap(i) for i in range(parts)]
    for copy in swaps:
        copy.start()

    scale = math.log2(math.e) / math.sqrt(hd)
    own_at = pl.ds(pl.multiple_of(c * half, 128), half)
    sends = list(swaps)
    lane = lax.broadcasted_iota(jnp.int32, (rows, 128), 1)
    nt = (((1,), (1,)), ((), ()))

    def attend(st, first, end):
        def one(j, core, acc_store, st_ref):
            row0 = pl.multiple_of(st * tokens + core * rows, 16)
            q = q_ref[pl.ds(j * batch, batch), pl.ds(row0, rows), :].reshape(batch * rows, hd)
            t1 = (
                lax.dot_general(q, ck_ref[...], nt, preferred_element_type=jnp.float32) * scale
                + bias_ref[...]
            )
            t2 = (
                lax.dot_general(
                    q, sk_ref[own_at, :], nt, preferred_element_type=jnp.float32
                )
                * scale
            )
            row = lax.broadcasted_iota(jnp.int32, (batch, rows, half), 1) + row0
            col = lax.broadcasted_iota(jnp.int32, (batch, rows, half), 2) + c * half
            seen = row.reshape(batch * rows, half) >= col.reshape(batch * rows, half)
            t2 = jnp.where(seen, t2, HIDDEN)
            top = jnp.maximum(
                jnp.max(t1, axis=1, keepdims=True), jnp.max(t2, axis=1, keepdims=True)
            )
            top = jnp.maximum(top, FLOOR)
            p1, p2 = jnp.exp2(t1 - top), jnp.exp2(t2 - top)
            total = jnp.sum(p1, axis=1, keepdims=True) + jnp.sum(p2, axis=1, keepdims=True)
            acc = jnp.dot(
                p1.astype(jnp.bfloat16), cv_ref[...], preferred_element_type=jnp.float32
            ) + jnp.dot(
                p2.astype(jnp.bfloat16), sv_ref[own_at, :], preferred_element_type=jnp.float32
            )
            stat = st_ref[st]
            for b in range(batch):
                at = slice(b * rows, (b + 1) * rows)
                head = j * batch + b
                acc_store(pl.multiple_of(head * hd, 128), acc[at])
                stat = jnp.where(lane == head, top[at], stat)
                stat = jnp.where(lane == 64 + head, total[at], stat)
            st_ref[st] = stat

        def keep(at, acc):
            acc_own[st, :, pl.ds(at, hd)] = acc

        def give(at, acc):
            acc_send[st, :, pl.ds(at, hd)] = acc.astype(jnp.bfloat16)

        def body(j, carry):
            one(j, 1 - c, give, st_send)
            one(j, c, keep, st_own)
            return carry

        if first == 0:
            st_own[st] = jnp.zeros((rows, 128), jnp.float32)
            st_send[st] = jnp.zeros((rows, 128), jnp.float32)
        lax.fori_loop(first, end, body, 0)
        if end < blocks:
            return
        for buf, got, sems in ((acc_send, acc_recv, acc_sems), (st_send, st_recv, st_sems)):
            copy = remote(buf.at[st], got.at[st], sems.at[0, st], sems.at[1, st], core_peer)
            copy.start()
            sends.append(copy)

    def merge(st):
        for buf, got, sems in ((acc_send, acc_recv, acc_sems), (st_send, st_recv, st_sems)):
            remote(buf.at[st], got.at[st], sems.at[0, st], sems.at[1, st], core_peer).wait_recv()
        stat0, stat1 = st_own[st], st_recv[st]
        done = []
        for j in range(heads):
            top0, top1 = stat0[:, j : j + 1], stat1[:, j : j + 1]
            top = jnp.maximum(top0, top1)
            f0, f1 = jnp.exp2(top0 - top), jnp.exp2(top1 - top)
            inv = 1.0 / (stat0[:, 64 + j : 65 + j] * f0 + stat1[:, 64 + j : 65 + j] * f1)
            acc0 = acc_own[st, :, j * hd : (j + 1) * hd]
            acc1 = acc_recv[st, :, j * hd : (j + 1) * hd].astype(jnp.float32)
            done.append(((acc0 * (f0 * inv)) + (acc1 * (f1 * inv))).astype(jnp.bfloat16))
        for i in range(group_count):
            group = jnp.concatenate(done[i * nsec : (i + 1) * nsec], axis=1)
            moved = jnp.dot(group, perm_ref[...], preferred_element_type=jnp.float32).astype(
                jnp.bfloat16
            )
            for k in range(nsec):
                a_send[st, k, :, i * hd : (i + 1) * hd] = moved[:, k * hd : (k + 1) * hd]
        a_all[st, h, c, s] = a_send[st, s]
        for k in range(1, nsec):
            copy = remote(
                a_send.at[st, sec(k)], a_all.at[st, h, c, s],
                z_send.at[st, k - 1], z_recv.at[st, k - 1], z_peer(k),
            )
            copy.start()
            sends.append(copy)

    def forward(st):
        for k in range(1, nsec):
            remote(
                a_send.at[st, 0], a_all.at[st, h, c, sec(nsec - k)],
                z_send.at[st, k - 1], z_recv.at[st, k - 1], z_peer(k),
            ).wait_recv()
        held = a_all.at[st, h, c]
        for copy in (
            remote(held, held, x_sems.at[0, st], x_sems.at[1, st], x_peer),
            remote(held, held, core_send.at[st, 0], core_recv.at[st, 0], core_peer),
        ):
            copy.start()
            sends.append(copy)

    def share(st):
        held = a_all.at[st, 1 - h, c]
        remote(held, held, x_sems.at[0, st], x_sems.at[1, st], x_peer).wait_recv()
        copy = remote(held, held, core_send.at[st, 1], core_recv.at[st, 1], core_peer)
        copy.start()
        sends.append(copy)

    def pass_on(i):
        w_swap(i).wait_recv()
        copy = w_pass(i)
        copy.start()
        sends.append(copy)

    def ready(st):
        for i, which in enumerate((h, 1 - h)):
            held = a_all.at[st, which, 1 - c]
            remote(held, held, core_send.at[st, i], core_recv.at[st, i], core_peer).wait_recv()

    early, late = blocks // 6, 2 * blocks // 3
    attend(0, 0, blocks)
    attend(1, 0, early)
    merge(0)
    pass_on(0)
    attend(1, early, late)
    pass_on(1)
    forward(0)
    attend(1, late, blocks)
    pass_on(2)
    merge(1)
    share(0)
    w_own.wait()
    for i in range(parts):
        w_pass(i).wait_recv()
    ready(0)

    chunk = right_send.shape[2]
    chunks = ncols // chunk

    def product(st, which, n):
        at = pl.ds(pl.multiple_of(n * chunk, 128), chunk)
        total = jnp.zeros((tokens, chunk), jnp.float32)
        for hh in range(2):
            left = a_all[st, hh, :, which].reshape(tokens, depth)
            total += jnp.dot(left, w_all[hh, :, at], preferred_element_type=jnp.float32)
        return total

    last = nsec - 1
    ways = (
        (right_send, right_recv, r_ssem, r_rsem, s, 1, lambda i: last - i),
        (left_send, left_recv, l_ssem, l_rsem, last - s, -1, lambda i: i),
    )

    def hop(way, m):
        out, got, ssem, rsem, _, step, _ = way
        to = (g, jnp.clip(s + step, 0, last), c, h)
        return remote(out.at[m], got.at[m], ssem.at[m], rsem.at[m], to)

    per_stage = last * chunks

    def valid(m, behind):
        return (m >= 0) & (m < stages * per_stage) & ((m // chunks) % last < last - behind)

    def wave(t, carry):
        for way in ways:
            out, got, _, _, behind, _, owner = way
            m = t - behind

            @pl.when(valid(m, behind))
            def _():
                total = product(m // per_stage, owner((m // chunks) % last), m % chunks)

                @pl.when(behind == 0)
                def _():
                    out[m] = total.astype(jnp.bfloat16)

                @pl.when(behind > 0)
                def _():
                    hop(way, m).wait_recv()
                    out[m] = (total + got[m].astype(jnp.float32)).astype(jnp.bfloat16)

                @pl.when(valid(m - 2, behind))
                def _():
                    hop(way, m - 2).wait_send()

                hop(way, m).start()

        return carry

    lax.fori_loop(0, per_stage // 3, wave, 0)
    forward(1)
    lax.fori_loop(per_stage // 3, 2 * per_stage // 3, wave, 0)
    share(1)
    lax.fori_loop(2 * per_stage // 3, per_stage, wave, 0)
    ready(1)
    lax.fori_loop(per_stage, stages * per_stage + last, wave, 0)

    for st in range(stages):
        for n in range(chunks):
            kept[...] = product(st, s, n)
            for way in ways:
                got, behind = way[1], way[4]
                m = st * per_stage + (last - behind) * chunks + n

                @pl.when(behind > 0)
                def _():
                    hop(way, m).wait_recv()
                    kept[...] += got[m].astype(jnp.float32)

            out_ref[st * tokens : (st + 1) * tokens, n * chunk : (n + 1) * chunk] = kept[
                ...
            ].astype(jnp.bfloat16)

    def drain(m, carry):
        for way in ways:
            behind = way[4]

            @pl.when(valid(m, behind) & jnp.logical_not(valid(m + 2, behind)))
            def _():
                hop(way, m).wait_send()

        return carry

    lax.fori_loop(0, stages * per_stage, drain, 0)
    for copy in sends:
        copy.wait_send()


def fused(queries, slice_kv, cache_keys, cache_values, block_table, slice_index, out_weight):
    slice_len, heads, hd = queries.shape
    nsec = lax.axis_size("section")
    stages = 2
    half = slice_len // 2
    rows = half // stages
    width = heads * hd
    ncols = out_weight.shape[2] // 2
    depth = out_weight.shape[0] * out_weight.shape[1]
    chunk = ncols // 2
    items = stages * (nsec - 1) * (ncols // chunk)
    live = live_keys(block_table, slice_index, cache_keys.shape[2], cache_keys.shape[1])
    bias = jnp.where(live, 0.0, HIDDEN).astype(jnp.float32)[None, :]
    piece = hd // nsec
    perm = np.zeros((nsec, nsec, piece, nsec, nsec, piece), np.float32)
    for head in range(nsec):
        for part in range(nsec):
            for r in range(piece):
                perm[head, part, r, part, head, r] = 1.0
    perm = jnp.asarray(perm.reshape(nsec * hd, nsec * hd), jnp.bfloat16)
    bf16, f32 = jnp.bfloat16, jnp.float32
    dma = pltpu.SemaphoreType.DMA
    vmem = pl.BlockSpec(memory_space=pltpu.VMEM)
    return pl.pallas_call(
        functools.partial(kernel, (slice_len, heads, hd, nsec, stages)),
        out_shape=jax.ShapeDtypeStruct((slice_len, ncols), bf16),
        in_specs=[vmem] * 7 + [pl.BlockSpec(memory_space=pl.ANY)],
        out_specs=vmem,
        scratch_shapes=[
            pltpu.VMEM((2, depth, ncols), bf16),
            pltpu.VMEM((stages, 2, 2, nsec, rows, depth), bf16),
            pltpu.VMEM((stages, nsec, rows, depth), bf16),
            pltpu.VMEM((stages, rows, width), f32),
            pltpu.VMEM((stages, rows, width), bf16),
            pltpu.VMEM((stages, rows, width), bf16),
            pltpu.VMEM((stages, rows, 128), f32),
            pltpu.VMEM((stages, rows, 128), f32),
            pltpu.VMEM((stages, rows, 128), f32),
            *[pltpu.VMEM((items, 2 * rows, chunk), bf16)] * 4,
            pltpu.VMEM((2 * rows, chunk), f32),
            dma,
            dma((4, 3)),
            dma((2, stages)),
            dma((2, stages)),
            dma((stages, nsec - 1)),
            dma((stages, nsec - 1)),
            dma((2, stages)),
            dma((stages, 2)),
            dma((stages, 2)),
            *[dma((items,))] * 4,
        ],
        compiler_params=pltpu.CompilerParams(
            collective_id=0, has_side_effects=True, vmem_limit_bytes=52 * 1024 * 1024
        ),
    )(
        jnp.swapaxes(queries, 0, 1),
        cache_keys.reshape(-1, hd),
        cache_values.reshape(-1, hd),
        slice_kv[:, 0],
        slice_kv[:, 1],
        bias,
        perm,
        out_weight.reshape(depth, -1),
    )


def on_device(*arrays):
    slice_len, heads, hd = arrays[0].shape
    nsec = lax.axis_size("section")
    fits = (
        lax.axis_size("ctx") == 2
        and lax.axis_size("head") == 2
        and lax.axis_size("group") == 2
        and arrays[6].shape[0] * arrays[6].shape[1] % 96 == 0
        and hd == 128
        and slice_len % 256 == 0
        and heads % nsec == 0
        and heads % 4 == 0
        and heads <= 64
        and arrays[6].shape[2] % 512 == 0
    )
    return fused(*arrays) if fits else plain(*arrays)


def solution(mesh):
    placed = (
        P(("group", "section"), "head", None),
        P(("group", "section"), None, None),
        P(("group", "section"), "ctx", None, None),
        P(("group", "section"), "ctx", None, None),
        P("group", None),
        P("group"),
        P("head", "section", "ctx"),
    )
    return jax.shard_map(
        on_device,
        mesh=mesh,
        in_specs=placed,
        out_specs=P(("group", "section"), ("ctx", "head")),
        check_vma=False,
    )
```
